512 devices in a mesh: ctx: 16 (over y, core), resp: 8 (over x, z_lo), head: 4 (over z_hi).
Axes of the slice: x: 4, y: 8, z: 8 (z_hi: 4, z_lo: 2; z = z_hi * 2 + z_lo), core: 2. Of those that a mesh axis runs over, the one named last changes fastest.
Arguments:
- queries: bfloat16 [32768, 64, 128], P(('ctx', 'resp'), 'head'), may hold values from -6 to 6, as said below
- prompt_k: bfloat16 [1536, 8, 128], P(('ctx', 'resp'), 'head'), may hold values from -6 to 6, as said below
- prompt_v: bfloat16 [1536, 8, 128], P(('ctx', 'resp'), 'head'), may hold values from -6 to 6
- resp_k: bfloat16 [32768, 8, 128], P(('ctx', 'resp'), 'head'), may hold values from -6 to 6
- resp_v: bfloat16 [32768, 8, 128], P(('ctx', 'resp'), 'head'), may hold values from -6 to 6
- prefix_k: bfloat16 [64, 8, 128], P(None, 'head'), may hold values from -6 to 6
- prefix_v: bfloat16 [64, 8, 128], P(None, 'head'), may hold values from -6 to 6
- d_out: bfloat16 [32768, 64, 128], P(('ctx', 'resp'), 'head'), may hold values from -6 to 6
- shard_mask: int32 [128, 128], P(('ctx', 'resp')), may hold values from 0 to 1, as said below
- resp_lengths: int32 [128], P(('ctx', 'resp')), may hold values from 1 to 256, 16512 in all
- prefix_count: int32 [1], replicated, may hold values from 32 to 64
Outputs:
- attn_out: bfloat16 [32768, 64, 128], P(('ctx', 'resp'), 'head')
- grad_prefix_k: float32 [64, 8, 128], P(None, 'head')
- grad_prefix_v: float32 [64, 8, 128], P(None, 'head')
The draws below stay inside these ranges and needn't reach their ends.
Inputs may be any that keep to these rules, and one draw needn't show every extreme that they name: `queries`: of order one; rows may be strongly aligned with one another. `prompt_k`: of order one; rows may be strongly aligned with one another. `resp_lengths`: the lengths sum to 16512 and the largest is exactly 256. `shard_mask`: each response attends to a window of 64 consecutive prompt blocks (block-sparse sliding-window prompt attention, no wrap) and no other.
All inputs are finite; a program needn't handle non-finite values. No bound on the sum of `resp_lengths` on one device may be relied on, other than what follows from the above.
Results may differ from the reference program's by a relative error of at most 0.013.
Values may be sent and summed in bfloat16 or wider, within the bound.
A program may use at most 128 MiB of HBM per device.

```python
import math
import jax
import jax.numpy as jnp
import numpy as np
from jax import lax

H = 64
KVH = 8
HD = 128
PREFIX = 64
RLEN = 256
PROMPT_DEV = 12
NBLK = 128
RESPONSES = 128
RTOK = 32768
PROMPT = 1536


def draw_queries(key, part):
    key = jax.random.fold_in(key, 11)
    drawn = jnp.clip(jax.random.normal(key, (RTOK, H, HD), jnp.float32), -6.0, 6.0)
    return drawn.astype(jnp.bfloat16)


def draw_prompt_k(key, part):
    key = jax.random.fold_in(key, 12)
    drawn = jnp.clip(jax.random.normal(key, (PROMPT, KVH, HD), jnp.float32), -6.0, 6.0)
    return drawn.astype(jnp.bfloat16)


def draw_shard_mask(key, part):
    key = jax.random.fold_in(key, 13)
    window = NBLK // 2
    starts = jax.random.randint(key, (RESPONSES,), 0, NBLK - window + 1)
    blocks = jnp.arange(NBLK, dtype=jnp.int32)[None, :]
    inside = (blocks >= starts[:, None]) & (blocks < starts[:, None] + window)
    return inside.astype(jnp.int32)


def block_scale(rng, dims, pieces, smallest, top_value):
    level, own = 1.0, jax.random.fold_in(rng, 6)
    for dim, parts in pieces:
        steps = jnp.exp(jax.random.uniform(jax.random.fold_in(own, dim), (parts,), jnp.float32, smallest / len(pieces), top_value / len(pieces)))
        level = level * jnp.repeat(steps, dims[dim] // parts).reshape([-1 if axis == dim else 1 for axis in range(len(dims))])
    return level


def length_profile(amount, total, reach, slope):
    portions = [(1 << 20) // math.isqrt(grade ** slope) + 1 for grade in range(2, amount + 1)]
    rest, holding = total - reach - (amount - 1), [1] * (amount - 1)
    while rest > 0:
        free = [i for i in range(amount - 1) if holding[i] < reach]
        pool, budget = sum([portions[i] for i in free]), rest
        for i in free:
            extra = min(reach - holding[i], max(1, budget * portions[i] // pool), rest)
            holding[i] = holding[i] + extra
            rest = rest - extra
    return np.array([reach] + holding)


def uneven(key, amount, total, most, slope):
    if amount == 2:
        one = jax.random.randint(key, (), max(1, total - most), min(most, total - 1) + 1)
        return jnp.stack([one, total - one])
    tallies = jnp.asarray(length_profile(amount, total, most, slope), jnp.int32)
    twos = (amount - 1) // 2
    donor, sink = tallies[1:1 + 2 * twos:2], tallies[2:2 + 2 * twos:2]
    room = jnp.minimum(donor - 1, most - sink)
    shifted = jax.random.randint(jax.random.fold_in(key, 1), (twos,), 0, 1 << 20) % (room + 1)
    tallies = tallies.at[1:1 + 2 * twos:2].set(donor - shifted).at[2:2 + 2 * twos:2].set(sink + shifted)
    return tallies[jax.random.permutation(jax.random.fold_in(key, 2), amount)]


def gaussian(rng, dims, scale, reach, shards=(), kind=jnp.bfloat16):
    level = block_scale(rng, dims, shards, -0.22, 0.18) if shards else 1.0
    values = jax.random.normal(rng, dims, jnp.float32) * scale * level
    return jnp.minimum(jnp.maximum(values, -reach), reach).astype(kind)


def setup_inputs(seed: int = 0) -> dict:
    streams_of = jax.random.split(jax.random.key(seed), 12)
    return {
        "queries": draw_queries(jax.random.fold_in(streams_of[11], 71), 0),
        "prompt_k": draw_prompt_k(jax.random.fold_in(streams_of[11], 71), 0),
        "prompt_v": gaussian(streams_of[2], (PROMPT, KVH, HD), 1.0, 6.0, ((0, 128), (1, 4))),
        "resp_k": gaussian(streams_of[3], (RTOK, KVH, HD), 1.0, 6.0, ((0, 128), (1, 4))),
        "resp_v": gaussian(streams_of[4], (RTOK, KVH, HD), 1.0, 6.0, ((0, 128), (1, 4))),
        "prefix_k": gaussian(streams_of[5], (PREFIX, KVH, HD), 1.0, 6.0, ((1, 4),)),
        "prefix_v": gaussian(streams_of[6], (PREFIX, KVH, HD), 1.0, 6.0, ((1, 4),)),
        "d_out": gaussian(streams_of[7], (RTOK, H, HD), 1.0, 6.0, ((0, 128), (1, 4))),
        "shard_mask": draw_shard_mask(jax.random.fold_in(streams_of[11], 71), 0),
        "resp_lengths": uneven(streams_of[9], RESPONSES, RESPONSES * RLEN // 2 + RLEN // 2, RLEN, 1).astype(jnp.int32),
        "prefix_count": jax.random.randint(streams_of[10], (1,), PREFIX // 2, PREFIX + 1).astype(jnp.int32),
    }


def reference(queries, prompt_k, prompt_v, resp_k, resp_v, prefix_k, prefix_v, d_out, shard_mask, resp_lengths, prefix_count):
    q_group = H // KVH
    score_scale = HD ** -0.5
    highest = lax.Precision.HIGHEST
    positions = jnp.arange(RLEN, dtype=jnp.int32)
    live_slots = jnp.arange(PREFIX, dtype=jnp.int32) < prefix_count[0]

    def one_response(carried, resp_index):
        grad_k, grad_v = carried
        row_start = (resp_index * RLEN).astype(jnp.int32)
        resp_queries = lax.dynamic_slice_in_dim(queries, row_start, RLEN, 0).reshape(RLEN, KVH, q_group, HD)
        own_keys = lax.dynamic_slice_in_dim(resp_k, row_start, RLEN, 0)
        own_values = lax.dynamic_slice_in_dim(resp_v, row_start, RLEN, 0)
        grad_in = lax.dynamic_slice_in_dim(d_out, row_start, RLEN, 0).reshape(RLEN, KVH, q_group, HD)
        length_now = resp_lengths[resp_index]
        all_keys = jnp.concatenate([prefix_k, prompt_k, own_keys], axis=0).astype(jnp.float32)
        all_values = jnp.concatenate([prefix_v, prompt_v, own_values], axis=0).astype(jnp.float32)
        prompt_seen = jnp.repeat(shard_mask[resp_index], PROMPT_DEV) == 1
        own_seen = (positions[None, :] <= positions[:, None]) & (positions[None, :] < length_now)
        key_mask = jnp.concatenate([
            jnp.broadcast_to(live_slots[None, :], (RLEN, PREFIX)),
            jnp.broadcast_to(prompt_seen[None, :], (RLEN, PROMPT)),
            own_seen], axis=1)
        scores = jnp.einsum("tgqd,kgd->tgqk", resp_queries.astype(jnp.float32), all_keys, precision=highest) * score_scale
        scores = jnp.where(key_mask[:, None, None, :], scores, -jnp.inf)
        row_max = jnp.max(scores, axis=-1)
        expo = jnp.exp(scores - row_max[..., None])
        row_total = jnp.sum(expo, axis=-1)
        weights = (expo / row_total[..., None]).astype(jnp.bfloat16)
        mixed = jnp.einsum("tgqk,kgd->tgqd", weights.astype(jnp.float32), all_values, precision=highest)
        valid_rows = (positions < length_now).astype(jnp.float32)
        grad_rows = grad_in.astype(jnp.float32) * valid_rows[:, None, None, None]
        inner_dot = jnp.sum(grad_rows * mixed, axis=-1)
        exact_pre = expo[..., :PREFIX] / row_total[..., None]
        d_pre = jnp.einsum("tgqd,jgd->tgqj", grad_rows, prefix_v.astype(jnp.float32), precision=highest)
        d_scores = exact_pre * (d_pre - inner_dot[..., None])
        grad_v = grad_v + jnp.einsum("tgqj,tgqd->jgd", exact_pre, grad_rows, precision=highest)
        grad_k = grad_k + jnp.einsum("tgqj,tgqd->jgd", d_scores, resp_queries.astype(jnp.float32), precision=highest) * score_scale
        return (grad_k, grad_v), mixed.reshape(RLEN, H, HD).astype(jnp.bfloat16)

    zeros_grad = jnp.zeros((PREFIX, KVH, HD), jnp.float32)
    (grad_prefix_k, grad_prefix_v), outputs = lax.scan(one_response, (zeros_grad, zeros_grad), jnp.arange(RESPONSES, dtype=jnp.int32))
    attn_out = outputs.reshape(RTOK, H, HD)
    return attn_out, grad_prefix_k, grad_prefix_v
```

```python
import functools
import math

import jax
import jax.numpy as jnp
from jax import lax
from jax.experimental import pallas as pl
from jax.experimental.pallas import tpu as pltpu
from jax.sharding import PartitionSpec as P

MESH = pl.DeviceIdType.MESH
f32, bf16 = jnp.float32, jnp.bfloat16
NEG = -1e30
NY, NX = 8, 4
BLOCK = 12
WINDOW = 64
R = 256
ROWS = 4096
TOKENS = R // 16
CHUNKS = ROWS // R
C = math.log2(math.e) / math.sqrt(128.0)


def dot_t(a, b):
    return lax.dot_general(a, b, (((1,), (1,)), ((), ())), preferred_element_type=f32)


def dot(a, b):
    return lax.dot_general(a, b, (((1,), (0,)), ((), ())), preferred_element_type=f32)


def dot_0(a, b):
    return lax.dot_general(a, b, (((0,), (0,)), ((), ())), preferred_element_type=f32)


def pick(x):
    x = x.reshape(TOKENS, 2, 8, 256)
    return jnp.concatenate([x[:, 0:1, :, :128], x[:, 1:2, :, 128:]], axis=1).reshape(R, 128)


def kernel(
    q_hbm, g_hbm, rk_ref, rv_ref, pk_ref, pv_ref, sk_ref, sv_ref, mask_ref, len_ref, cnt_ref,
    out_hbm, gk_ref, gv_ref,
    tmp, kx, vx, dv, q_ref, g_ref, o_ref, qe, ge, m1, l1, a1, e0, d0, wk, wv,
    gat, part, r1, r2, fin, acc_k, acc_v,
    in_sem, out_sem, z_send, z_recv, y_send, y_recv, x_send, x_recv, s_send, s_recv,
    r1_send, r1_recv, r2_send, r2_recv, r3_send, r3_recv,
):
    ctx, resp = lax.axis_index("ctx"), lax.axis_index("resp")
    y, core = ctx // 2, ctx % 2
    x, z = resp // 2, resp % 2

    q_copy = pltpu.make_async_copy(q_hbm, q_ref, in_sem.at[0])
    g_copy = pltpu.make_async_copy(g_hbm, g_ref, in_sem.at[1])
    q_copy.start()
    g_copy.start()

    barrier = pltpu.get_barrier_semaphore()

    def greet_ctx(k, c):
        pl.semaphore_signal(barrier, inc=1, device_id={"ctx": (ctx + k) % 16}, device_id_type=MESH)
        return c

    def greet_resp(k, c):
        pl.semaphore_signal(barrier, inc=1, device_id={"resp": (resp + k) % 8}, device_id_type=MESH)
        return c

    lax.fori_loop(1, 16, greet_ctx, 0)
    lax.fori_loop(1, 8, greet_resp, 0)

    def load2(ref, n):
        tmp[pl.ds(0, 2 * n), :] = ref[...].astype(f32)
        return tmp[pl.ds(0, n, stride=2), :], tmp[pl.ds(1, n, stride=2), :]

    k0, k1 = load2(sk_ref, BLOCK)
    v0, v1 = load2(sv_ref, BLOCK)
    mine = jnp.concatenate(
        [k0[:8], k1[:8], v0[:8], v1[:8], k0[8:], k1[8:], v0[8:], v1[8:]], axis=0
    ).astype(bf16)
    gat[ctx * 8 + resp] = mine

    pl.semaphore_wait(barrier, 22)

    def z_copy():
        b = ctx * 8 + resp
        return pltpu.make_async_remote_copy(
            src_ref=gat.at[b], dst_ref=gat.at[b], send_sem=z_send.at[0], recv_sem=z_recv.at[0],
            device_id={"resp": x * 2 + 1 - z}, device_id_type=MESH,
        )

    def y_copy(k):
        pair = gat.at[pl.ds(ctx * 8 + x * 2, 2)]
        return pltpu.make_async_remote_copy(
            src_ref=pair, dst_ref=pair, send_sem=y_send.at[k], recv_sem=y_recv.at[k],
            device_id={"ctx": ((y + k) % NY) * 2 + core}, device_id_type=MESH,
        )

    def x_copy(k, j):
        pair = gat.at[pl.ds(((y + NY - k) % NY) * 16 + core * 8 + x * 2, 2)]
        return pltpu.make_async_remote_copy(
            src_ref=pair, dst_ref=pair, send_sem=x_send.at[k, j], recv_sem=x_recv.at[k, j],
            device_id={"resp": ((x + j) % NX) * 2 + z}, device_id_type=MESH,
        )

    def s_copy(k):
        line = gat.at[pl.ds(((y + NY - k) % NY) * 16 + core * 8, 8)]
        return pltpu.make_async_remote_copy(
            src_ref=line, dst_ref=line, send_sem=s_send.at[k], recv_sem=s_recv.at[k],
            device_id={"ctx": y * 2 + 1 - core}, device_id_type=MESH,
        )

    z_copy().start()

    def both(ref, n):
        return jnp.concatenate(load2(ref, n), axis=1).astype(bf16)

    pk2, pv2 = both(pk_ref, 64), both(pv_ref, 64)
    z2 = jnp.zeros_like(pk2)
    kx[pl.ds(0, 64), :] = pk2
    kx[pl.ds(64, 64), :] = pk2
    vx[pl.ds(0, 64), :] = pv2
    vx[pl.ds(64, 64), :] = z2
    dv[pl.ds(0, 64), :] = z2
    dv[pl.ds(64, 64), :] = pv2
    kx[pl.ds(128, 256), :] = both(rk_ref, 256)
    vx[pl.ds(128, 256), :] = both(rv_ref, 256)
    length, count = len_ref[0], cnt_ref[0]
    lane = lax.broadcasted_iota(jnp.int32, (R, 128), 1)
    row = lax.broadcasted_iota(jnp.int32, (R, 1), 0)
    tok = lax.shift_right_logical(row, 4)
    head_hi = jnp.where((row & 8) == 8, 1.0, 0.0).astype(f32)
    hi = jnp.broadcast_to(head_hi, (R, 128)).astype(bf16)
    lo = jnp.broadcast_to(1.0 - head_hi, (R, 128)).astype(bf16)

    def own(i, nk):
        rows = pl.ds(pl.multiple_of(i * R, R), R)
        q = q_ref[rows, :]
        q2 = jnp.concatenate([q * lo, q * hi], axis=1)
        qe[rows, :] = q2
        t = tok + i * TOKENS
        live = jnp.where(t < length, 1.0, 0.0)
        g = (g_ref[rows, :].astype(f32) * live).astype(bf16)
        g2 = jnp.concatenate([g * lo, g * hi], axis=1)
        ge[rows, :] = g2
        s = dot_t(q2, kx[pl.ds(0, 128 + nk), :])
        last = jnp.minimum(t, length - 1)
        parts = [jnp.where((lane & 63) < count, s[:, :128], NEG)]
        for j in range(nk // 128):
            parts.append(jnp.where(lane + j * 128 <= last, s[:, 128 + j * 128 : 256 + j * 128], NEG))
        s = jnp.concatenate(parts, axis=1)
        m = jnp.max(s, axis=1, keepdims=True)
        p = jnp.exp2((s - m) * C)
        first = p[:, :128]
        tot = jnp.where(lane < 64, first, 0.0)
        for j in range(nk // 128):
            tot = tot + p[:, 128 + j * 128 : 256 + j * 128]
        l1[rows, :] = tot
        m1[rows, :] = m
        e0[rows, :] = first
        a1[rows, :] = pick(dot(p.astype(bf16), vx[pl.ds(0, 128 + nk), :]))
        d = dot_t(g2, dv[...])
        d0[rows, :] = jnp.where(lane < 64, 1.0, d)

    def run_own(lo_i, hi_i, nk):
        lax.fori_loop(lo_i, hi_i, lambda i, c: (own(i, nk), c)[1], 0)

    q_copy.wait()
    g_copy.wait()
    run_own(0, 1, 128)
    z_copy().wait()

    def start_y(k, c):
        y_copy(k).start()
        return c

    lax.fori_loop(1, NY, start_y, 0)
    for j in range(1, NX):
        x_copy(0, j).start()
    run_own(1, 4, 128)

    def pass_x(k, c):
        y_copy(k).wait_recv()
        for j in range(1, NX):
            x_copy(k, j).start()
        return c

    lax.fori_loop(1, NY, pass_x, 0)
    run_own(4, 8, 128)
    run_own(8, 12, 256)

    def pass_s(k, c):
        for j in range(1, NX):
            x_copy(k, j).wait_recv()
        s_copy(k).start()
        return c

    lax.fori_loop(0, NY, pass_s, 0)
    run_own(12, 16, 256)

    def end_gather(k, c):
        s_copy(k).wait()
        for j in range(1, NX):
            x_copy(k, j).wait_send()
        return c

    lax.fori_loop(0, NY, end_gather, 0)

    def end_y(k, c):
        y_copy(k).wait_send()
        return c

    lax.fori_loop(1, NY, end_y, 0)

    block_ids = lax.broadcasted_iota(jnp.int32, (1, 128), 1)
    first_block = jnp.min(jnp.where(mask_ref[...] == 1, block_ids, WINDOW))
    win = gat[pl.ds(first_block, WINDOW)].astype(f32)
    wk[pl.ds(0, 512), :] = jnp.concatenate([win[:, 0:8], win[:, 8:16]], axis=2).reshape(512, 256).astype(bf16)
    wv[pl.ds(0, 512), :] = jnp.concatenate([win[:, 16:24], win[:, 24:32]], axis=2).reshape(512, 256).astype(bf16)

    low4 = lax.broadcasted_iota(jnp.int32, (32, 8, 128), 1) < 4

    def rest(part4):
        part4 = part4.reshape(32, 2, 8, 128)
        b0, b1 = part4[:, 0], part4[:, 1]
        left = jnp.where(low4, b0, pltpu.roll(b1, 4, 1))
        right = jnp.where(low4, pltpu.roll(b0, 4, 1), b1)
        return jnp.concatenate([left, right], axis=2).reshape(256, 256).astype(bf16)

    wk[pl.ds(512, 256), :] = rest(win[:, 32:40])
    wv[pl.ds(512, 256), :] = rest(win[:, 40:48])

    acc_k[...] = jnp.zeros_like(acc_k)
    acc_v[...] = jnp.zeros_like(acc_v)

    def out_copy(i):
        rows = pl.ds(pl.multiple_of(i * R, R), R)
        return pltpu.make_async_copy(o_ref.at[rows], out_hbm.at[rows], out_sem.at[i])

    def prompt(i, c):
        rows = pl.ds(pl.multiple_of(i * R, R), R)
        q2, g2 = qe[rows, :], ge[rows, :]
        s = dot_t(q2, wk[...])
        mo = m1[rows, :]
        m = jnp.maximum(mo, jnp.max(s, axis=1, keepdims=True))
        p = jnp.exp2((s - m) * C)
        alpha = jnp.exp2((mo - m) * C)
        tot = l1[rows, :] * alpha
        for j in range(6):
            tot = tot + p[:, j * 128 : (j + 1) * 128]
        inv = 1.0 / jnp.sum(tot, axis=1, keepdims=True)
        mixed = (a1[rows, :] * alpha + pick(dot(p.astype(bf16), wv[...]))) * inv
        o_ref[rows, :] = mixed.astype(bf16)
        out_copy(i).start()
        g = (g2[:, :128] + g2[:, 128:]).astype(f32)
        inner = jnp.sum(g * mixed, axis=1, keepdims=True)
        ed = e0[rows, :] * (alpha * inv) * (d0[rows, :] - jnp.where(lane < 64, 0.0, inner))
        ed = ed.astype(bf16)
        acc_v[...] += dot_0(ed, g2)[:64]
        acc_k[...] += dot_0(ed, q2)[64:]
        return c

    lax.fori_loop(0, CHUNKS, prompt, 0)

    part[pl.ds(0, 4)] = acc_k[:, :128].astype(bf16).reshape(4, 16, 128)
    part[pl.ds(4, 4)] = acc_k[:, 128:].astype(bf16).reshape(4, 16, 128)
    part[pl.ds(8, 4)] = acc_v[:, :128].astype(bf16).reshape(4, 16, 128)
    part[pl.ds(12, 4)] = acc_v[:, 128:].astype(bf16).reshape(4, 16, 128)

    def r1_copy(k):
        to = (ctx + k) % 16
        return pltpu.make_async_remote_copy(
            src_ref=part.at[to], dst_ref=r1.at[k], send_sem=r1_send.at[k], recv_sem=r1_recv.at[k],
            device_id={"ctx": to}, device_id_type=MESH,
        )

    def r2_copy(k):
        return pltpu.make_async_remote_copy(
            src_ref=r2.at[resp], dst_ref=r2.at[resp], send_sem=r2_send.at[k], recv_sem=r2_recv.at[k],
            device_id={"resp": (resp + k) % 8}, device_id_type=MESH,
        )

    def r3_copy(k):
        return pltpu.make_async_remote_copy(
            src_ref=fin.at[ctx], dst_ref=fin.at[ctx], send_sem=r3_send.at[k], recv_sem=r3_recv.at[k],
            device_id={"ctx": (ctx + k) % 16}, device_id_type=MESH,
        )

    def each(copy, n, what):
        def step(k, c):
            getattr(copy(k), what)()
            return c

        lax.fori_loop(1, n, step, 0)

    each(r1_copy, 16, "start")
    total = part[ctx].astype(f32)
    each(r1_copy, 16, "wait_recv")
    for k in range(1, 16):
        total = total + r1[k].astype(f32)
    r2[resp] = total
    each(r2_copy, 8, "start")
    each(r2_copy, 8, "wait_recv")
    total = r2[0]
    for k in range(1, 8):
        total = total + r2[k]
    fin[ctx] = total
    each(r3_copy, 16, "start")
    each(r3_copy, 16, "wait_recv")
    for head in range(2):
        dst = pl.ds(head, 64, stride=2)
        gk_ref[dst, :] = fin[pl.ds(4 * head, 4)].reshape(64, 128) * (128.0 ** (-0.5))
        gv_ref[dst, :] = fin[pl.ds(8 + 4 * head, 4)].reshape(64, 128)
    each(r1_copy, 16, "wait_send")
    each(r2_copy, 8, "wait_send")
    each(r3_copy, 16, "wait_send")

    def end_out(i, c):
        out_copy(i).wait()
        return c

    lax.fori_loop(0, CHUNKS, end_out, 0)


def per_device(
    queries, prompt_k, prompt_v, resp_k, resp_v, prefix_k, prefix_v, d_out, shard_mask, resp_lengths, prefix_count
):
    vm = pl.BlockSpec(memory_space=pltpu.VMEM)
    sm = pl.BlockSpec(memory_space=pltpu.SMEM)
    hbm = pl.BlockSpec(memory_space=pl.ANY)
    vmem, dma = pltpu.VMEM, pltpu.SemaphoreType.DMA
    out, gk, gv = pl.pallas_call(
        kernel,
        out_shape=[
            jax.ShapeDtypeStruct((ROWS, 128), bf16),
            jax.ShapeDtypeStruct((128, 128), f32),
            jax.ShapeDtypeStruct((128, 128), f32),
        ],
        in_specs=[hbm, hbm] + [vm] * 7 + [sm, sm],
        out_specs=[hbm, vm, vm],
        scratch_shapes=[
            vmem((512, 128), f32), vmem((384, 256), bf16), vmem((384, 256), bf16), vmem((128, 256), bf16),
            vmem((ROWS, 128), bf16), vmem((ROWS, 128), bf16), vmem((ROWS, 128), bf16),
            vmem((ROWS, 256), bf16), vmem((ROWS, 256), bf16),
            vmem((ROWS, 1), f32), vmem((ROWS, 128), f32), vmem((ROWS, 128), f32),
            vmem((ROWS, 128), f32), vmem((ROWS, 128), f32),
            vmem((768, 256), bf16), vmem((768, 256), bf16),
            vmem((128, 48, 128), bf16),
            vmem((16, 16, 128), bf16), vmem((16, 16, 128), bf16), vmem((8, 16, 128), f32), vmem((16, 16, 128), f32),
            vmem((64, 256), f32), vmem((64, 256), f32),
            dma((2,)), dma((CHUNKS,)), dma((1,)), dma((1,)), dma((8,)), dma((8,)), dma((8, 4)), dma((8, 4)),
            dma((8,)), dma((8,)), dma((16,)), dma((16,)), dma((8,)), dma((8,)), dma((16,)), dma((16,)),
        ],
        compiler_params=pltpu.CompilerParams(
            collective_id=0, has_side_effects=True, vmem_limit_bytes=48 << 20
        ),
    )(
        queries.reshape(ROWS, 128), d_out.reshape(ROWS, 128), resp_k.reshape(512, 128), resp_v.reshape(512, 128),
        prefix_k.reshape(128, 128), prefix_v.reshape(128, 128), prompt_k.reshape(2 * BLOCK, 128),
        prompt_v.reshape(2 * BLOCK, 128), shard_mask, resp_lengths, prefix_count,
    )
    return out.reshape(256, 16, 128), gk.reshape(64, 2, 128), gv.reshape(64, 2, 128)


def solution(mesh):
    tokens = P(("ctx", "resp"), "head", None)
    prefix = P(None, "head", None)
    in_specs = (
        tokens, tokens, tokens, tokens, tokens, prefix, prefix, tokens,
        P(("ctx", "resp"), None), P(("ctx", "resp")), P(),
    )
    return jax.shard_map(
        per_device, mesh=mesh, in_specs=in_specs, out_specs=(tokens, prefix, prefix), check_vma=False
    )
```

```python
import functools
import math

import jax
import jax.numpy as jnp
from jax import lax
from jax.experimental import pallas as pl
from jax.experimental.pallas import tpu as pltpu
from jax.sharding import PartitionSpec as P

MESH = pl.DeviceIdType.MESH
f32, bf16 = jnp.float32, jnp.bfloat16
NEG = -1e30
NY, NX = 8, 4
BLOCK = 12
WINDOW = 64
R = 512
ROWS = 4096
TOKENS = R // 16
CHUNKS = ROWS // R
C = math.log2(math.e) / math.sqrt(128.0)


def dot_t(a, b):
    return lax.dot_general(a, b, (((1,), (1,)), ((), ())), preferred_element_type=f32)


def dot(a, b):
    return lax.dot_general(a, b, (((1,), (0,)), ((), ())), preferred_element_type=f32)


def dot_0(a, b):
    return lax.dot_general(a, b, (((0,), (0,)), ((), ())), preferred_element_type=f32)


def pick(x):
    x = x.reshape(TOKENS, 2, 8, 256)
    return jnp.concatenate([x[:, 0:1, :, :128], x[:, 1:2, :, 128:]], axis=1).reshape(R, 128)


def kernel(
    q_hbm, g_hbm, rk_hbm, rv_hbm, pk_hbm, pv_hbm, sk_hbm, sv_hbm, mask_hbm, len_hbm, cnt_hbm,
    o_ref, gk_ref, gv_ref,
    tmp, kx, vx, dv, q_ref, g_ref, rk_ref, rv_ref, pk_ref, pv_ref, sk_ref, sv_ref,
    mask_ref, len_ref, cnt_ref, qe, ge, m1, l1, a1, e0, d0, wk, wv,
    s1, s2, m2, gat, part, r1, r2, fin, acc_k, acc_v,
    in_sem, y_send, y_recv, x_send, x_recv, s_send, s_recv,
    r1_send, r1_recv, r2_send, r2_recv, r3_send, r3_recv,
):
    ctx, resp = lax.axis_index("ctx"), lax.axis_index("resp")
    y, core = ctx // 2, ctx % 2
    x, z = resp // 2, resp % 2

    loads = [
        pltpu.make_async_copy(src, dst, in_sem.at[n])
        for n, (src, dst) in enumerate(
            [
                (sk_hbm, sk_ref), (sv_hbm, sv_ref), (pk_hbm, pk_ref), (pv_hbm, pv_ref), (rk_hbm, rk_ref),
                (rv_hbm, rv_ref), (len_hbm, len_ref), (cnt_hbm, cnt_ref), (mask_hbm, mask_ref),
                (q_hbm, q_ref), (g_hbm, g_ref),
            ]
        )
    ]
    for load in loads:
        load.start()

    barrier = pltpu.get_barrier_semaphore()

    def peer_xzc(k):
        i = (resp * 2 + core + k) % 16
        return {"ctx": y * 2 + i % 2, "resp": i // 2}

    def peer_yz(k, j):
        return {"ctx": ((y + k) % NY) * 2 + core, "resp": x * 2 + (z + j) % 2}

    def greet_xzc(k, c):
        pl.semaphore_signal(barrier, inc=1, device_id=peer_xzc(k), device_id_type=MESH)
        return c

    def greet_yz(k, c):
        for j in range(2):
            pl.semaphore_signal(barrier, inc=1, device_id=peer_yz(k, j), device_id_type=MESH)
        return c

    lax.fori_loop(1, NY, greet_yz, 0)
    lax.fori_loop(1, 16, greet_xzc, 0)

    def load2(ref, n):
        tmp[pl.ds(0, 2 * n), :] = ref[...].astype(f32)
        return tmp[pl.ds(0, n, stride=2), :], tmp[pl.ds(1, n, stride=2), :]

    for load in loads[:2]:
        load.wait()
    k0, k1 = load2(sk_ref, BLOCK)
    v0, v1 = load2(sv_ref, BLOCK)
    mine = jnp.concatenate(
        [k0[:8], k1[:8], v0[:8], v1[:8], k0[8:], k1[8:], v0[8:], v1[8:]], axis=0
    ).astype(bf16)
    gat[ctx * 8 + resp] = mine

    def both(ref, n):
        return jnp.concatenate(load2(ref, n), axis=1).astype(bf16)

    for load in loads[2:9]:
        load.wait()
    pk2, pv2 = both(pk_ref, 64), both(pv_ref, 64)
    z2 = jnp.zeros_like(pk2)
    kx[pl.ds(0, 64), :] = pk2
    kx[pl.ds(64, 64), :] = pk2
    vx[pl.ds(0, 64), :] = pv2
    vx[pl.ds(64, 64), :] = z2
    dv[pl.ds(0, 64), :] = z2
    dv[pl.ds(64, 64), :] = pv2
    kx[pl.ds(128, 256), :] = both(rk_ref, 256)
    vx[pl.ds(128, 256), :] = both(rv_ref, 256)
    length, count = len_ref[0], cnt_ref[0]
    lane = lax.broadcasted_iota(jnp.int32, (R, 128), 1)
    row = lax.broadcasted_iota(jnp.int32, (R, 1), 0)
    tok = lax.shift_right_logical(row, 4)
    head_hi = jnp.where((row & 8) == 8, 1.0, 0.0).astype(f32)
    hi = jnp.broadcast_to(head_hi, (R, 128)).astype(bf16)
    lo = jnp.broadcast_to(1.0 - head_hi, (R, 128)).astype(bf16)

    def own_scores(i, nk, slot):
        rows = pl.ds(pl.multiple_of(i * R, R), R)
        q = q_ref[rows, :]
        q2 = jnp.concatenate([q * lo, q * hi], axis=1)
        qe[rows, :] = q2
        last = jnp.minimum(tok + i * TOKENS, length - 1)
        s = dot_t(q2, kx[pl.ds(0, 128 + nk), :])
        parts = [jnp.where((lane & 63) < count, s[:, :128], NEG)]
        for j in range(nk // 128):
            parts.append(jnp.where(lane + j * 128 <= last, s[:, 128 + j * 128 : 256 + j * 128], NEG))
        top = parts[0]
        for piece in parts[1:]:
            top = jnp.maximum(top, piece)
        m1[rows, :] = jnp.max(top, axis=1, keepdims=True)
        for j, piece in enumerate(parts):
            s1[slot, :, pl.ds(j * 128, 128)] = piece

    def own_values(i, nk, slot):
        rows = pl.ds(pl.multiple_of(i * R, R), R)
        live = jnp.where(tok + i * TOKENS < length, 1.0, 0.0)
        g = (g_ref[rows, :].astype(f32) * live).astype(bf16)
        g2 = jnp.concatenate([g * lo, g * hi], axis=1)
        ge[rows, :] = g2
        p = jnp.exp2((s1[slot, :, pl.ds(0, 128 + nk)] - m1[rows, :]) * C)
        first = p[:, :128]
        tot = jnp.where(lane < 64, first, 0.0)
        for j in range(nk // 128):
            tot = tot + p[:, 128 + j * 128 : 256 + j * 128]
        l1[rows, :] = tot
        e0[rows, :] = first
        a1[rows, :] = pick(dot(p.astype(bf16), vx[pl.ds(0, 128 + nk), :]))
        d0[rows, :] = jnp.where(lane < 64, 1.0, dot_t(g2, dv[...]))

    def staggered(scores, values, first, last):
        scores(first, 0)

        def two(j, c):
            i = first + 2 * j
            scores(i + 1, 1)
            values(i, 0)
            scores(i + 2, 0)
            values(i + 1, 1)
            return c

        lax.fori_loop(0, (last - first) // 2 - 1, two, 0)
        scores(last - 1, 1)
        values(last - 2, 0)
        values(last - 1, 1)

    def run_own(first, last, nk):
        staggered(lambda i, slot: own_scores(i, nk, slot), lambda i, slot: own_values(i, nk, slot), first, last)

    for load in loads[9:]:
        load.wait()
    run_own(0, CHUNKS // 2, 128)

    pl.semaphore_wait(barrier, 29)

    def y_copy(k, j):
        b = ctx * 8 + resp
        return pltpu.make_async_remote_copy(
            src_ref=gat.at[b], dst_ref=gat.at[b], send_sem=y_send.at[k, j], recv_sem=y_recv.at[k, j],
            device_id=peer_yz(k, j), device_id_type=MESH,
        )

    def x_copy(k, j):
        pair = gat.at[pl.ds(((y + NY - k) % NY) * 16 + core * 8 + x * 2, 2)]
        return pltpu.make_async_remote_copy(
            src_ref=pair, dst_ref=pair, send_sem=x_send.at[k, j], recv_sem=x_recv.at[k, j],
            device_id={"resp": ((x + j) % NX) * 2 + z}, device_id_type=MESH,
        )

    def s_copy(k):
        line = gat.at[pl.ds(((y + NY - k) % NY) * 16 + core * 8, 8)]
        return pltpu.make_async_remote_copy(
            src_ref=line, dst_ref=line, send_sem=s_send.at[k], recv_sem=s_recv.at[k],
            device_id={"ctx": y * 2 + 1 - core}, device_id_type=MESH,
        )

    def near_first(n):
        return lax.rem((n + 1) // 2 * (n % 2) + (NY - n // 2) * (1 - n % 2), NY)

    y_copy(0, 1).start()

    def start_y(n, c):
        k = near_first(n)
        y_copy(k, 0).start()
        y_copy(k, 1).start()
        return c

    lax.fori_loop(1, NY, start_y, 0)

    def pass_x(n, c):
        k = near_first(n)
        y_copy(k, 1).wait_recv()

        @pl.when(n > 0)
        def _():
            y_copy(k, 0).wait_recv()

        for j in (1, 3, 2):
            x_copy(k, j).start()
        return c

    def pass_s(n, c):
        k = near_first(n)
        for j in range(1, NX):
            x_copy(k, j).wait_recv()
        s_copy(k).start()
        return c

    run_own(CHUNKS // 2, CHUNKS, 256)
    lax.fori_loop(0, NY, pass_x, 0)
    lax.fori_loop(0, NY, pass_s, 0)

    def end_gather(k, c):
        s_copy(k).wait()
        for j in range(1, NX):
            x_copy(k, j).wait_send()
        y_copy(k, 1).wait_send()

        @pl.when(k > 0)
        def _():
            y_copy(k, 0).wait_send()

        return c

    lax.fori_loop(0, NY, end_gather, 0)

    block_ids = lax.broadcasted_iota(jnp.int32, (1, 128), 1)
    first_block = jnp.min(jnp.where(mask_ref[...] == 1, block_ids, WINDOW))
    win = gat[pl.ds(first_block, WINDOW)].astype(f32)
    wk[pl.ds(0, 512), :] = jnp.concatenate([win[:, 0:8], win[:, 8:16]], axis=2).reshape(512, 256).astype(bf16)
    wv[pl.ds(0, 512), :] = jnp.concatenate([win[:, 16:24], win[:, 24:32]], axis=2).reshape(512, 256).astype(bf16)

    low4 = lax.broadcasted_iota(jnp.int32, (32, 8, 128), 1) < 4

    def rest(part4):
        part4 = part4.reshape(32, 2, 8, 128)
        b0, b1 = part4[:, 0], part4[:, 1]
        left = jnp.where(low4, b0, pltpu.roll(b1, 4, 1))
        right = jnp.where(low4, pltpu.roll(b0, 4, 1), b1)
        return jnp.concatenate([left, right], axis=2).reshape(256, 256).astype(bf16)

    wk[pl.ds(512, 256), :] = rest(win[:, 32:40])
    wv[pl.ds(512, 256), :] = rest(win[:, 40:48])

    acc_k[...] = jnp.zeros_like(acc_k)
    acc_v[...] = jnp.zeros_like(acc_v)

    def prompt_scores(i, slot):
        rows = pl.ds(pl.multiple_of(i * R, R), R)
        s = dot_t(qe[rows, :], wk[...])
        s2[slot] = s
        top = s[:, :128]
        for j in range(1, 6):
            top = jnp.maximum(top, s[:, j * 128 : (j + 1) * 128])
        m2[slot] = jnp.maximum(m1[rows, :], jnp.max(top, axis=1, keepdims=True))

    def prompt_values(i, slot):
        rows = pl.ds(pl.multiple_of(i * R, R), R)
        q2, g2 = qe[rows, :], ge[rows, :]
        mo, m = m1[rows, :], m2[slot]
        p = jnp.exp2((s2[slot] - m) * C)
        alpha = jnp.exp2((mo - m) * C)
        tot = l1[rows, :] * alpha
        for j in range(6):
            tot = tot + p[:, j * 128 : (j + 1) * 128]
        inv = 1.0 / jnp.sum(tot, axis=1, keepdims=True)
        mixed = (a1[rows, :] * alpha + pick(dot(p.astype(bf16), wv[...]))) * inv
        o_ref[rows, :] = mixed.astype(bf16)
        g = (g2[:, :128] + g2[:, 128:]).astype(f32)
        inner = jnp.sum(g * mixed, axis=1, keepdims=True)
        ed = e0[rows, :] * (alpha * inv) * (d0[rows, :] - jnp.where(lane < 64, 0.0, inner))
        ed = ed.astype(bf16)
        acc_v[...] += dot_0(ed, g2)[:64]
        acc_k[...] += dot_0(ed, q2)[64:]

    staggered(prompt_scores, prompt_values, 0, CHUNKS)

    part[pl.ds(0, 4)] = acc_k[:, :128].astype(bf16).reshape(4, 16, 128)
    part[pl.ds(4, 4)] = acc_k[:, 128:].astype(bf16).reshape(4, 16, 128)
    part[pl.ds(8, 4)] = acc_v[:, :128].astype(bf16).reshape(4, 16, 128)
    part[pl.ds(12, 4)] = acc_v[:, 128:].astype(bf16).reshape(4, 16, 128)

    seat = resp * 2 + core

    def r1_copy(k):
        return pltpu.make_async_remote_copy(
            src_ref=part.at[(seat + k) % 16], dst_ref=r1.at[k], send_sem=r1_send.at[k], recv_sem=r1_recv.at[k],
            device_id=peer_xzc(k), device_id_type=MESH,
        )

    def r2_copy(k):
        return pltpu.make_async_remote_copy(
            src_ref=r2.at[y], dst_ref=r2.at[y], send_sem=r2_send.at[k], recv_sem=r2_recv.at[k],
            device_id=peer_yz(k, 0), device_id_type=MESH,
        )

    def r3_copy(k):
        return pltpu.make_async_remote_copy(
            src_ref=fin.at[seat], dst_ref=fin.at[seat], send_sem=r3_send.at[k], recv_sem=r3_recv.at[k],
            device_id=peer_xzc(k), device_id_type=MESH,
        )

    def each(copy, n, what):
        def step(k, c):
            getattr(copy(k), what)()
            return c

        lax.fori_loop(1, n, step, 0)

    each(r1_copy, 16, "start")
    total = part[seat].astype(f32)
    each(r1_copy, 16, "wait_recv")
    for k in range(1, 16):
        total = total + r1[k].astype(f32)
    r2[y] = total
    each(r2_copy, 8, "start")
    each(r2_copy, 8, "wait_recv")
    total = r2[0]
    for k in range(1, 8):
        total = total + r2[k]
    fin[seat] = total
    each(r3_copy, 16, "start")
    each(r3_copy, 16, "wait_recv")
    for head in range(2):
        dst = pl.ds(head, 64, stride=2)
        gk_ref[dst, :] = fin[pl.ds(4 * head, 4)].reshape(64, 128) * (128.0 ** (-0.5))
        gv_ref[dst, :] = fin[pl.ds(8 + 4 * head, 4)].reshape(64, 128)
    each(r1_copy, 16, "wait_send")
    each(r2_copy, 8, "wait_send")
    each(r3_copy, 16, "wait_send")


def place(o_ref, k_ref, v_ref, out_ref, gk_ref, gv_ref, sem):
    n = ROWS // 4
    copies = [pltpu.make_async_copy(k_ref, gk_ref, sem.at[4]), pltpu.make_async_copy(v_ref, gv_ref, sem.at[5])]
    for i in range(4):
        rows = pl.ds(i * n, n)
        copies.append(pltpu.make_async_copy(o_ref.at[rows], out_ref.at[rows], sem.at[i]))
    for copy in copies:
        copy.start()
    for copy in copies:
        copy.wait()


def per_device(
    queries, prompt_k, prompt_v, resp_k, resp_v, prefix_k, prefix_v, d_out, shard_mask, resp_lengths, prefix_count
):
    vm = pl.BlockSpec(memory_space=pltpu.VMEM)
    hbm = pl.BlockSpec(memory_space=pltpu.HBM)
    vmem, dma = pltpu.VMEM, pltpu.SemaphoreType.DMA
    out, gk, gv = pl.pallas_call(
        kernel,
        out_shape=[vmem((ROWS, 128), bf16), vmem((128, 128), f32), vmem((128, 128), f32)],
        in_specs=[hbm] * 11,
        out_specs=[vm] * 3,
        scratch_shapes=[
            vmem((512, 128), f32), vmem((384, 256), bf16), vmem((384, 256), bf16), vmem((128, 256), bf16),
            vmem((ROWS, 128), bf16), vmem((ROWS, 128), bf16), vmem((512, 128), bf16), vmem((512, 128), bf16),
            vmem((128, 128), bf16), vmem((128, 128), bf16), vmem((2 * BLOCK, 128), bf16), vmem((2 * BLOCK, 128), bf16),
            vmem((1, 128), jnp.int32), pltpu.SMEM((1,), jnp.int32), pltpu.SMEM((1,), jnp.int32),
            vmem((ROWS, 256), bf16), vmem((ROWS, 256), bf16),
            vmem((ROWS, 1), f32), vmem((ROWS, 128), f32), vmem((ROWS, 128), f32),
            vmem((ROWS, 128), f32), vmem((ROWS, 128), f32),
            vmem((768, 256), bf16), vmem((768, 256), bf16),
            vmem((2, R, 384), f32), vmem((2, R, 768), f32), vmem((2, R, 1), f32),
            vmem((128, 48, 128), bf16),
            vmem((16, 16, 128), bf16), vmem((16, 16, 128), bf16), vmem((8, 16, 128), f32), vmem((16, 16, 128), f32),
            vmem((64, 256), f32), vmem((64, 256), f32),
            dma((11,)), dma((8, 2)), dma((8, 2)), dma((8, 4)), dma((8, 4)),
            dma((8,)), dma((8,)), dma((16,)), dma((16,)), dma((8,)), dma((8,)), dma((16,)), dma((16,)),
        ],
        compiler_params=pltpu.CompilerParams(
            collective_id=0, has_side_effects=True, vmem_limit_bytes=60 << 20
        ),
    )(
        queries.reshape(ROWS, 128), d_out.reshape(ROWS, 128), resp_k.reshape(512, 128), resp_v.reshape(512, 128),
        prefix_k.reshape(128, 128), prefix_v.reshape(128, 128), prompt_k.reshape(2 * BLOCK, 128),
        prompt_v.reshape(2 * BLOCK, 128), shard_mask, resp_lengths, prefix_count,
    )
    out, gk, gv = pl.pallas_call(
        place,
        out_shape=[
            jax.ShapeDtypeStruct((ROWS, 128), bf16),
            jax.ShapeDtypeStruct((128, 128), f32),
            jax.ShapeDtypeStruct((128, 128), f32),
        ],
        in_specs=[vm] * 3,
        out_specs=[hbm] * 3,
        scratch_shapes=[dma((6,))],
        compiler_params=pltpu.CompilerParams(vmem_limit_bytes=16 << 20),
    )(out, gk, gv)
    return out.reshape(256, 16, 128), gk.reshape(64, 2, 128), gv.reshape(64, 2, 128)


def solution(mesh):
    tokens = P(("ctx", "resp"), "head", None)
    prefix = P(None, "head", None)
    in_specs = (
        tokens, tokens, tokens, tokens, tokens, prefix, prefix, tokens,
        P(("ctx", "resp"), None), P(("ctx", "resp")), P(),
    )
    return jax.shard_map(
        per_device, mesh=mesh, in_specs=in_specs, out_specs=(tokens, prefix, prefix), check_vma=False
    )
```

```python
import functools
import math

import jax
import jax.numpy as jnp
from jax import lax
from jax.experimental import pallas as pl
from jax.experimental.pallas import tpu as pltpu
from jax.sharding import PartitionSpec as P

MESH = pl.DeviceIdType.MESH
f32, bf16 = jnp.float32, jnp.bfloat16
NEG = -1e30
NY, NX = 8, 4
BLOCK = 12
WINDOW = 64
R = 1024
NEAR = 4
ROWS = 4096
TOKENS = R // 16
CHUNKS = ROWS // R
C = math.log2(math.e) / math.sqrt(128.0)


def dot_t(a, b):
    return lax.dot_general(a, b, (((1,), (1,)), ((), ())), preferred_element_type=f32)


def dot(a, b):
    return lax.dot_general(a, b, (((1,), (0,)), ((), ())), preferred_element_type=f32)


def dot_0(a, b):
    return lax.dot_general(a, b, (((0,), (0,)), ((), ())), preferred_element_type=f32)


def pick(x):
    x = x.reshape(TOKENS, 2, 8, 256)
    return jnp.concatenate([x[:, 0:1, :, :128], x[:, 1:2, :, 128:]], axis=1).reshape(R, 128)


def kernel(
    q_hbm, g_hbm, rk_hbm, rv_hbm, pk_hbm, pv_hbm, sk_hbm, sv_hbm, mask_hbm, len_hbm, cnt_hbm,
    o_ref, gk_ref, gv_ref,
    tmp, kx, vx, dv, q_ref, g_ref, rk_ref, rv_ref, pk_ref, pv_ref, sk_ref, sv_ref,
    mask_ref, len_ref, cnt_ref, qe, ge, m1, l1, a1, e0, d0, wk, wv,
    s1, s2, m2, gat, part, r1, r2, fin, acc_k, acc_v,
    in_sem, y_send, y_recv, x_send, x_recv, z_send, z_recv, s_send, s_recv,
    r1_send, r1_recv, r2_send, r2_recv, r3_send, r3_recv,
):
    ctx, resp = lax.axis_index("ctx"), lax.axis_index("resp")
    y, core = ctx // 2, ctx % 2
    x, z = resp // 2, resp % 2

    loads = [
        pltpu.make_async_copy(src, dst, in_sem.at[n])
        for n, (src, dst) in enumerate(
            [
                (sk_hbm, sk_ref), (sv_hbm, sv_ref), (pk_hbm, pk_ref), (pv_hbm, pv_ref), (rk_hbm, rk_ref),
                (rv_hbm, rv_ref), (len_hbm, len_ref), (cnt_hbm, cnt_ref), (mask_hbm, mask_ref),
                (q_hbm, q_ref), (g_hbm, g_ref),
            ]
        )
    ]
    for load in loads:
        load.start()

    barrier = pltpu.get_barrier_semaphore()

    def peer_xzc(k):
        i = (resp * 2 + core + k) % 16
        return {"ctx": y * 2 + i % 2, "resp": i // 2}

    def peer_yz(k, j):
        return {"ctx": ((y + k) % NY) * 2 + core, "resp": x * 2 + (z + j) % 2}

    def greet_xzc(k, c):
        pl.semaphore_signal(barrier, inc=1, device_id=peer_xzc(k), device_id_type=MESH)
        return c

    def greet_yz(k, c):
        for j in range(2):
            pl.semaphore_signal(barrier, inc=1, device_id=peer_yz(k, j), device_id_type=MESH)
        return c

    lax.fori_loop(1, NY, lambda i, c: greet_yz(lax.rem(i + 2, NY) + (i + 2) // NY, c), 0)
    lax.fori_loop(1, 16, lambda i, c: greet_xzc(lax.rem(i + 7, 16) + (i + 7) // 16, c), 0)

    def load2(ref, n):
        tmp[pl.ds(0, 2 * n), :] = ref[...].astype(f32)
        return tmp[pl.ds(0, n, stride=2), :], tmp[pl.ds(1, n, stride=2), :]

    for load in loads[:2]:
        load.wait()
    k0, k1 = load2(sk_ref, BLOCK)
    v0, v1 = load2(sv_ref, BLOCK)
    mine = jnp.concatenate(
        [k0[:8], k1[:8], v0[:8], v1[:8], k0[8:], k1[8:], v0[8:], v1[8:]], axis=0
    ).astype(bf16)
    gat[ctx * 8 + resp] = mine

    def both(ref, n):
        return jnp.concatenate(load2(ref, n), axis=1).astype(bf16)

    for load in loads[2:9]:
        load.wait()
    pk2, pv2 = both(pk_ref, 64), both(pv_ref, 64)
    z2 = jnp.zeros_like(pk2)
    kx[pl.ds(0, 64), :] = pk2
    kx[pl.ds(64, 64), :] = pk2
    vx[pl.ds(0, 64), :] = pv2
    vx[pl.ds(64, 64), :] = z2
    dv[pl.ds(0, 64), :] = z2
    dv[pl.ds(64, 64), :] = pv2
    kx[pl.ds(128, 256), :] = both(rk_ref, 256)
    vx[pl.ds(128, 256), :] = both(rv_ref, 256)
    length, count = len_ref[0], cnt_ref[0]
    lane = lax.broadcasted_iota(jnp.int32, (R, 128), 1)
    row = lax.broadcasted_iota(jnp.int32, (R, 1), 0)
    tok = lax.shift_right_logical(row, 4)
    head_hi = jnp.where((row & 8) == 8, 1.0, 0.0).astype(f32)
    hi = jnp.broadcast_to(head_hi, (R, 128)).astype(bf16)
    lo = jnp.broadcast_to(1.0 - head_hi, (R, 128)).astype(bf16)

    def own_scores(i, nk, slot):
        rows = pl.ds(pl.multiple_of(i * R, R), R)
        q = q_ref[rows, :]
        q2 = jnp.concatenate([q * lo, q * hi], axis=1)
        qe[rows, :] = q2
        last = jnp.minimum(tok + i * TOKENS, length - 1)
        s = dot_t(q2, kx[pl.ds(0, 128 + nk), :])
        parts = [jnp.where((lane & 63) < count, s[:, :128], NEG)]
        for j in range(nk // 128):
            parts.append(jnp.where(lane + j * 128 <= last, s[:, 128 + j * 128 : 256 + j * 128], NEG))
        top = parts[0]
        for piece in parts[1:]:
            top = jnp.maximum(top, piece)
        m1[rows, :] = jnp.broadcast_to(jnp.max(top, axis=1, keepdims=True), (R, 128))
        for j, piece in enumerate(parts):
            s1[slot, :, pl.ds(j * 128, 128)] = piece

    def own_values(i, nk, slot):
        rows = pl.ds(pl.multiple_of(i * R, R), R)
        live = jnp.where(tok + i * TOKENS < length, 1.0, 0.0)
        g = (g_ref[rows, :].astype(f32) * live).astype(bf16)
        g2 = jnp.concatenate([g * lo, g * hi], axis=1)
        ge[rows, :] = g2
        m = m1[rows, :]
        cols = [jnp.exp2((s1[slot, :, pl.ds(j * 128, 128)] - m) * C) for j in range(1 + nk // 128)]
        p = jnp.concatenate(cols, axis=1)
        first = p[:, :128]
        tot = jnp.where(lane < 64, first, 0.0)
        for j in range(nk // 128):
            tot = tot + p[:, 128 + j * 128 : 256 + j * 128]
        l1[rows, :] = tot
        e0[rows, :] = first
        a1[rows, :] = pick(dot(p.astype(bf16), vx[pl.ds(0, 128 + nk), :]))
        d0[rows, :] = jnp.where(lane < 64, 1.0, dot_t(g2, dv[...]))

    def staggered(scores, values, first, last):
        scores(first, 0)

        def two(j, c):
            i = first + 2 * j
            scores(i + 1, 1)
            values(i, 0)
            scores(i + 2, 0)
            values(i + 1, 1)
            return c

        lax.fori_loop(0, (last - first) // 2 - 1, two, 0)
        scores(last - 1, 1)
        values(last - 2, 0)
        values(last - 1, 1)

    def run_own(first, last, nk):
        staggered(lambda i, slot: own_scores(i, nk, slot), lambda i, slot: own_values(i, nk, slot), first, last)

    for load in loads[9:]:
        load.wait()
    run_own(0, CHUNKS // 2, 128)

    pl.semaphore_wait(barrier, 29)

    def remote(ref, sems, at, peer):
        return pltpu.make_async_remote_copy(
            src_ref=ref, dst_ref=ref, send_sem=sems[0].at[at], recv_sem=sems[1].at[at],
            device_id=peer, device_id_type=MESH,
        )

    def line(k):
        return ((y + NY - k) % NY) * 16 + core * 8

    def y_copy(k, j):
        return remote(gat.at[ctx * 8 + resp], (y_send, y_recv), (k, j), peer_yz(k, j))

    def x_copy(k, j, n):
        first = line(k) + x * 2
        ref = gat.at[pl.ds(first, 2)] if n == 2 else gat.at[pl.ds(first + z, 1)]
        return remote(ref, (x_send, x_recv), (k, j), {"resp": ((x + j) % NX) * 2 + z})

    def z_copy(k, j):
        ref = gat.at[line(k) + ((x + NX - j) % NX) * 2 + z]
        return remote(ref, (z_send, z_recv), (k, j), {"resp": x * 2 + 1 - z})

    def s_copy(k):
        return remote(gat.at[pl.ds(line(k), 8)], (s_send, s_recv), (k,), {"ctx": y * 2 + 1 - core})

    def at_distance(n):
        return lax.rem((n + 1) // 2 * (n % 2) + (NY - n // 2) * (1 - n % 2), NY)

    def loop(first, last, step):
        def body(n, c):
            step(at_distance(n))
            return c

        lax.fori_loop(first, last, body, 0)

    def send_near(k):
        for j in (2, 1, 3):
            x_copy(k, j, 1).start()
        z_copy(k, 0).start()

    def pass_near(k):
        y_copy(k, 0).wait_recv()
        send_near(k)

    def pass_far(k):
        for j in range(2):
            y_copy(k, j).wait_recv()
        for j in (2, 1, 3):
            x_copy(k, j, 2).start()

    def pass_z(k):
        for j in (1, 3, 2):
            x_copy(k, j, 1).wait_recv()
            z_copy(k, j).start()

    def line_near(k):
        for j in range(NX):
            z_copy(k, j).wait_recv()
        s_copy(k).start()

    def line_far(k):
        for j in (1, 3, 2):
            x_copy(k, j, 2).wait_recv()
        s_copy(k).start()

    def start_far(n, c):
        k = at_distance(NY - 1 - n)
        for j in range(2):
            y_copy(k, j).start()
        return c

    lax.fori_loop(0, NY - NEAR, start_far, 0)
    loop(1, NEAR, lambda k: y_copy(k, 0).start())
    send_near(0)
    run_own(CHUNKS // 2, CHUNKS, 256)
    loop(1, NEAR, pass_near)
    pass_z(0)
    loop(NEAR, NY, pass_far)
    loop(1, NEAR, pass_z)
    loop(0, NEAR, line_near)
    loop(NEAR, NY, line_far)

    def end_near(k):
        for j in range(1, NX):
            x_copy(k, j, 1).wait_send()
        for j in range(NX):
            z_copy(k, j).wait_send()
        s_copy(k).wait()

    def end_far(k):
        for j in range(2):
            y_copy(k, j).wait_send()
        for j in range(1, NX):
            x_copy(k, j, 2).wait_send()
        s_copy(k).wait()

    loop(1, NEAR, lambda k: y_copy(k, 0).wait_send())
    loop(0, NEAR, end_near)
    loop(NEAR, NY, end_far)

    block_ids = lax.broadcasted_iota(jnp.int32, (1, 128), 1)
    first_block = jnp.min(jnp.where(mask_ref[...] == 1, block_ids, WINDOW))
    win = gat[pl.ds(first_block, WINDOW)].astype(f32)
    wk[pl.ds(0, 512), :] = jnp.concatenate([win[:, 0:8], win[:, 8:16]], axis=2).reshape(512, 256).astype(bf16)
    wv[pl.ds(0, 512), :] = jnp.concatenate([win[:, 16:24], win[:, 24:32]], axis=2).reshape(512, 256).astype(bf16)

    low4 = lax.broadcasted_iota(jnp.int32, (32, 8, 128), 1) < 4

    def rest(part4):
        part4 = part4.reshape(32, 2, 8, 128)
        b0, b1 = part4[:, 0], part4[:, 1]
        left = jnp.where(low4, b0, pltpu.roll(b1, 4, 1))
        right = jnp.where(low4, pltpu.roll(b0, 4, 1), b1)
        return jnp.concatenate([left, right], axis=2).reshape(256, 256).astype(bf16)

    wk[pl.ds(512, 256), :] = rest(win[:, 32:40])
    wv[pl.ds(512, 256), :] = rest(win[:, 40:48])

    acc_k[...] = jnp.zeros_like(acc_k)
    acc_v[...] = jnp.zeros_like(acc_v)

    def prompt_scores(i, slot):
        rows = pl.ds(pl.multiple_of(i * R, R), R)
        s = dot_t(qe[rows, :], wk[...])
        s2[slot] = s
        top = s[:, :128]
        for j in range(1, 6):
            top = jnp.maximum(top, s[:, j * 128 : (j + 1) * 128])
        m2[slot] = jnp.maximum(m1[rows, :], jnp.broadcast_to(jnp.max(top, axis=1, keepdims=True), (R, 128)))

    def prompt_values(i, slot):
        rows = pl.ds(pl.multiple_of(i * R, R), R)
        q2, g2 = qe[rows, :], ge[rows, :]
        mo, m = m1[rows, :], m2[slot]
        cols = [jnp.exp2((s2[slot, :, pl.ds(j * 128, 128)] - m) * C) for j in range(6)]
        p = jnp.concatenate(cols, axis=1)
        alpha = jnp.exp2((mo - m) * C)
        tot = l1[rows, :] * alpha
        for j in range(6):
            tot = tot + p[:, j * 128 : (j + 1) * 128]
        inv = 1.0 / jnp.sum(tot, axis=1, keepdims=True)
        mixed = (a1[rows, :] * alpha + pick(dot(p.astype(bf16), wv[...]))) * inv
        o_ref[rows, :] = mixed.astype(bf16)
        g = (g2[:, :128] + g2[:, 128:]).astype(f32)
        inner = jnp.sum(g * mixed, axis=1, keepdims=True)
        ed = e0[rows, :] * (alpha * inv) * (d0[rows, :] - jnp.where(lane < 64, 0.0, inner))
        ed = ed.astype(bf16)
        acc_v[...] += dot_0(ed, g2)[:64]
        acc_k[...] += dot_0(ed, q2)[64:]

    staggered(prompt_scores, prompt_values, 0, CHUNKS)

    part[pl.ds(0, 4)] = acc_k[:, :128].astype(bf16).reshape(4, 16, 128)
    part[pl.ds(4, 4)] = acc_k[:, 128:].astype(bf16).reshape(4, 16, 128)
    part[pl.ds(8, 4)] = acc_v[:, :128].astype(bf16).reshape(4, 16, 128)
    part[pl.ds(12, 4)] = acc_v[:, 128:].astype(bf16).reshape(4, 16, 128)

    seat = resp * 2 + core

    def r1_copy(k):
        return pltpu.make_async_remote_copy(
            src_ref=part.at[(seat + k) % 16], dst_ref=r1.at[k], send_sem=r1_send.at[k], recv_sem=r1_recv.at[k],
            device_id=peer_xzc(k), device_id_type=MESH,
        )

    def r2_copy(k):
        return pltpu.make_async_remote_copy(
            src_ref=r2.at[y], dst_ref=r2.at[y], send_sem=r2_send.at[k], recv_sem=r2_recv.at[k],
            device_id=peer_yz(k, 0), device_id_type=MESH,
        )

    def r3_copy(k):
        return pltpu.make_async_remote_copy(
            src_ref=fin.at[seat], dst_ref=fin.at[seat], send_sem=r3_send.at[k], recv_sem=r3_recv.at[k],
            device_id=peer_xzc(k), device_id_type=MESH,
        )

    def each(copy, n, what):
        def step(i, c):
            getattr(copy(lax.rem(i + n // 2, n) + i // (n // 2)), what)()
            return c

        lax.fori_loop(0, n - 1, step, 0)

    each(r1_copy, 16, "start")
    total = part[seat].astype(f32)
    each(r1_copy, 16, "wait_recv")
    for k in range(1, 16):
        total = total + r1[k].astype(f32)
    r2[y] = total.astype(bf16)
    each(r2_copy, 8, "start")
    each(r2_copy, 8, "wait_recv")
    total = r2[0].astype(f32)
    for k in range(1, 8):
        total = total + r2[k].astype(f32)
    fin[seat] = total.astype(bf16)
    each(r3_copy, 16, "start")
    each(r3_copy, 16, "wait_recv")
    for head in range(2):
        dst = pl.ds(head, 64, stride=2)
        gk_ref[dst, :] = fin[pl.ds(4 * head, 4)].astype(f32).reshape(64, 128) * (128.0 ** (-0.5))
        gv_ref[dst, :] = fin[pl.ds(8 + 4 * head, 4)].astype(f32).reshape(64, 128)
    each(r1_copy, 16, "wait_send")
    each(r2_copy, 8, "wait_send")
    each(r3_copy, 16, "wait_send")


def place(o_ref, k_ref, v_ref, out_ref, gk_ref, gv_ref, sem):
    n = ROWS // 4
    copies = [pltpu.make_async_copy(k_ref, gk_ref, sem.at[4]), pltpu.make_async_copy(v_ref, gv_ref, sem.at[5])]
    for i in range(4):
        rows = pl.ds(i * n, n)
        copies.append(pltpu.make_async_copy(o_ref.at[rows], out_ref.at[rows], sem.at[i]))
    for copy in copies:
        copy.start()
    for copy in copies:
        copy.wait()


def per_device(
    queries, prompt_k, prompt_v, resp_k, resp_v, prefix_k, prefix_v, d_out, shard_mask, resp_lengths, prefix_count
):
    vm = pl.BlockSpec(memory_space=pltpu.VMEM)
    hbm = pl.BlockSpec(memory_space=pltpu.HBM)
    vmem, dma = pltpu.VMEM, pltpu.SemaphoreType.DMA
    out, gk, gv = pl.pallas_call(
        kernel,
        out_shape=[vmem((ROWS, 128), bf16), vmem((128, 128), f32), vmem((128, 128), f32)],
        in_specs=[hbm] * 11,
        out_specs=[vm] * 3,
        scratch_shapes=[
            vmem((512, 128), f32), vmem((384, 256), bf16), vmem((384, 256), bf16), vmem((128, 256), bf16),
            vmem((ROWS, 128), bf16), vmem((ROWS, 128), bf16), vmem((512, 128), bf16), vmem((512, 128), bf16),
            vmem((128, 128), bf16), vmem((128, 128), bf16), vmem((2 * BLOCK, 128), bf16), vmem((2 * BLOCK, 128), bf16),
            vmem((1, 128), jnp.int32), pltpu.SMEM((1,), jnp.int32), pltpu.SMEM((1,), jnp.int32),
            vmem((ROWS, 256), bf16), vmem((ROWS, 256), bf16),
            vmem((ROWS, 128), f32), vmem((ROWS, 128), f32), vmem((ROWS, 128), f32),
            vmem((ROWS, 128), f32), vmem((ROWS, 128), f32),
            vmem((768, 256), bf16), vmem((768, 256), bf16),
            vmem((2, R, 384), f32), vmem((2, R, 768), f32), vmem((2, R, 128), f32),
            vmem((128, 48, 128), bf16),
            vmem((16, 16, 128), bf16), vmem((16, 16, 128), bf16), vmem((8, 16, 128), bf16), vmem((16, 16, 128), bf16),
            vmem((64, 256), f32), vmem((64, 256), f32),
            dma((11,)), dma((8, 2)), dma((8, 2)), dma((8, 4)), dma((8, 4)), dma((8, 4)), dma((8, 4)),
            dma((8,)), dma((8,)), dma((16,)), dma((16,)), dma((8,)), dma((8,)), dma((16,)), dma((16,)),
        ],
        compiler_params=pltpu.CompilerParams(
            collective_id=0, has_side_effects=True, vmem_limit_bytes=60 << 20
        ),
    )(
        queries.reshape(ROWS, 128), d_out.reshape(ROWS, 128), resp_k.reshape(512, 128), resp_v.reshape(512, 128),
        prefix_k.reshape(128, 128), prefix_v.reshape(128, 128), prompt_k.reshape(2 * BLOCK, 128),
        prompt_v.reshape(2 * BLOCK, 128), shard_mask, resp_lengths, prefix_count,
    )
    out, gk, gv = pl.pallas_call(
        place,
        out_shape=[
            jax.ShapeDtypeStruct((ROWS, 128), bf16),
            jax.ShapeDtypeStruct((128, 128), f32),
            jax.ShapeDtypeStruct((128, 128), f32),
        ],
        in_specs=[vm] * 3,
        out_specs=[hbm] * 3,
        scratch_shapes=[dma((6,))],
        compiler_params=pltpu.CompilerParams(vmem_limit_bytes=16 << 20),
    )(out, gk, gv)
    return out.reshape(256, 16, 128), gk.reshape(64, 2, 128), gv.reshape(64, 2, 128)


def solution(mesh):
    tokens = P(("ctx", "resp"), "head", None)
    prefix = P(None, "head", None)
    in_specs = (
        tokens, tokens, tokens, tokens, tokens, prefix, prefix, tokens,
        P(("ctx", "resp"), None), P(("ctx", "resp")), P(),
    )
    return jax.shard_map(
        per_device, mesh=mesh, in_specs=in_specs, out_specs=(tokens, prefix, prefix), check_vma=False
    )
```

```python
import functools
import math

import jax
import jax.numpy as jnp
from jax import lax
from jax.experimental import pallas as pl
from jax.experimental.pallas import tpu as pltpu
from jax.sharding import PartitionSpec as P

MESH = pl.DeviceIdType.MESH
f32, bf16 = jnp.float32, jnp.bfloat16
NEG = -1e30
NY, NX = 8, 4
BLOCK = 12
WINDOW = 64
R = 1024
NEAR = 4
ROWS = 4096
TOKENS = R // 16
CHUNKS = ROWS // R
C = math.log2(math.e) / math.sqrt(128.0)


def dot_t(a, b):
    return lax.dot_general(a, b, (((1,), (1,)), ((), ())), preferred_element_type=f32)


def dot(a, b):
    return lax.dot_general(a, b, (((1,), (0,)), ((), ())), preferred_element_type=f32)


def pick(x):
    x = x.reshape(TOKENS, 2, 8, 256)
    return jnp.concatenate([x[:, 0:1, :, :128], x[:, 1:2, :, 128:]], axis=1).reshape(R, 128)


def kernel(
    q_hbm, g_hbm, rk_hbm, rv_hbm, pk_hbm, pv_hbm, sk_hbm, sv_hbm, mask_hbm, len_hbm, cnt_hbm,
    o_ref, gk_ref, gv_ref,
    tmp, kx, vx, dv, q_ref, g_ref, rk_ref, rv_ref, pk_ref, pv_ref, sk_ref, sv_ref,
    mask_ref, len_ref, cnt_ref, qe, ge, m1, l1, a1, e0, d0, wk, wv,
    s1, s2, m2, gat, part, r1, r2, fin, acc, turned,
    in_sem, y_send, y_recv, x_send, x_recv, z_send, z_recv, s_send, s_recv,
    r1_send, r1_recv, r2_send, r2_recv, r3_send, r3_recv,
):
    ctx, resp = lax.axis_index("ctx"), lax.axis_index("resp")
    y, core = ctx // 2, ctx % 2
    x, z = resp // 2, resp % 2

    loads = [
        pltpu.make_async_copy(src, dst, in_sem.at[n])
        for n, (src, dst) in enumerate(
            [
                (sk_hbm, sk_ref), (sv_hbm, sv_ref), (pk_hbm, pk_ref), (pv_hbm, pv_ref), (rk_hbm, rk_ref),
                (rv_hbm, rv_ref), (len_hbm, len_ref), (cnt_hbm, cnt_ref), (mask_hbm, mask_ref),
                (q_hbm, q_ref), (g_hbm, g_ref),
            ]
        )
    ]
    for load in loads:
        load.start()

    barrier = pltpu.get_barrier_semaphore()

    def peer_xzc(k):
        i = (resp * 2 + core + k) % 16
        return {"ctx": y * 2 + i % 2, "resp": i // 2}

    def peer_yz(k, j):
        return {"ctx": ((y + k) % NY) * 2 + core, "resp": x * 2 + (z + j) % 2}

    def greet_xzc(k, c):
        pl.semaphore_signal(barrier, inc=1, device_id=peer_xzc(k), device_id_type=MESH)
        return c

    def greet_yz(k, c):
        for j in range(2):
            pl.semaphore_signal(barrier, inc=1, device_id=peer_yz(k, j), device_id_type=MESH)
        return c

    lax.fori_loop(1, NY, lambda i, c: greet_yz(lax.rem(i + 2, NY) + (i + 2) // NY, c), 0)
    lax.fori_loop(1, 16, lambda i, c: greet_xzc(lax.rem(i + 7, 16) + (i + 7) // 16, c), 0)

    def load2(ref, n):
        tmp[pl.ds(0, 2 * n), :] = ref[...].astype(f32)
        return tmp[pl.ds(0, n, stride=2), :], tmp[pl.ds(1, n, stride=2), :]

    for load in loads[:2]:
        load.wait()
    k0, k1 = load2(sk_ref, BLOCK)
    v0, v1 = load2(sv_ref, BLOCK)
    mine = jnp.concatenate(
        [k0[:8], k1[:8], v0[:8], v1[:8], k0[8:], k1[8:], v0[8:], v1[8:]], axis=0
    ).astype(bf16)
    gat[ctx * 8 + resp] = mine

    def both(ref, n):
        return jnp.concatenate(load2(ref, n), axis=1).astype(bf16)

    for load in loads[2:9]:
        load.wait()
    pk2, pv2 = both(pk_ref, 64), both(pv_ref, 64)
    z2 = jnp.zeros_like(pk2)
    kx[pl.ds(0, 64), :] = pk2
    kx[pl.ds(64, 64), :] = pk2
    vx[pl.ds(0, 64), :] = pv2
    vx[pl.ds(64, 64), :] = z2
    dv[pl.ds(0, 64), :] = z2
    dv[pl.ds(64, 64), :] = pv2
    kx[pl.ds(128, 256), :] = both(rk_ref, 256)
    vx[pl.ds(128, 256), :] = both(rv_ref, 256)
    length, count = len_ref[0], cnt_ref[0]
    lane = lax.broadcasted_iota(jnp.int32, (R, 128), 1)
    row = lax.broadcasted_iota(jnp.int32, (R, 1), 0)
    tok = lax.shift_right_logical(row, 4)
    head_hi = jnp.where((row & 8) == 8, 1.0, 0.0).astype(f32)
    hi = jnp.broadcast_to(head_hi, (R, 128)).astype(bf16)
    lo = jnp.broadcast_to(1.0 - head_hi, (R, 128)).astype(bf16)

    def own_scores(i, nk, slot):
        rows = pl.ds(pl.multiple_of(i * R, R), R)
        q = q_ref[rows, :]
        q2 = jnp.concatenate([q * lo, q * hi], axis=1)
        qe[rows, :] = q2
        turned[128:, rows] = q.T
        last = jnp.minimum(tok + i * TOKENS, length - 1)
        s = dot_t(q2, kx[pl.ds(0, 128 + nk), :])
        parts = [jnp.where((lane & 63) < count, s[:, :128], NEG)]
        for j in range(nk // 128):
            parts.append(jnp.where(lane + j * 128 <= last, s[:, 128 + j * 128 : 256 + j * 128], NEG))
        top = parts[0]
        for piece in parts[1:]:
            top = jnp.maximum(top, piece)
        m1[rows, :] = jnp.broadcast_to(jnp.max(top, axis=1, keepdims=True), (R, 128))
        for j, piece in enumerate(parts):
            s1[slot, :, pl.ds(j * 128, 128)] = piece

    def own_values(i, nk, slot):
        rows = pl.ds(pl.multiple_of(i * R, R), R)
        live = jnp.where(tok + i * TOKENS < length, 1.0, 0.0)
        g = (g_ref[rows, :].astype(f32) * live).astype(bf16)
        g2 = jnp.concatenate([g * lo, g * hi], axis=1)
        ge[rows, :] = g2
        turned[:128, rows] = g.T
        m = m1[rows, :]
        cols = [jnp.exp2((s1[slot, :, pl.ds(j * 128, 128)] - m) * C) for j in range(1 + nk // 128)]
        p = jnp.concatenate(cols, axis=1)
        first = p[:, :128]
        tot = jnp.where(lane < 64, first, 0.0)
        for j in range(nk // 128):
            tot = tot + p[:, 128 + j * 128 : 256 + j * 128]
        l1[rows, :] = tot
        e0[rows, :] = first
        a1[rows, :] = pick(dot(p.astype(bf16), vx[pl.ds(0, 128 + nk), :]))
        d0[rows, :] = jnp.where(lane < 64, 1.0, dot_t(g2, dv[...]))

    def staggered(scores, values, first, last):
        scores(first, 0)

        def two(j, c):
            i = first + 2 * j
            scores(i + 1, 1)
            values(i, 0)
            scores(i + 2, 0)
            values(i + 1, 1)
            return c

        lax.fori_loop(0, (last - first) // 2 - 1, two, 0)
        scores(last - 1, 1)
        values(last - 2, 0)
        values(last - 1, 1)

    def run_own(first, last, nk):
        staggered(lambda i, slot: own_scores(i, nk, slot), lambda i, slot: own_values(i, nk, slot), first, last)

    for load in loads[9:]:
        load.wait()
    run_own(0, CHUNKS // 2, 128)

    pl.semaphore_wait(barrier, 29)

    def remote(ref, sems, at, peer):
        return pltpu.make_async_remote_copy(
            src_ref=ref, dst_ref=ref, send_sem=sems[0].at[at], recv_sem=sems[1].at[at],
            device_id=peer, device_id_type=MESH,
        )

    def line(k):
        return ((y + NY - k) % NY) * 16 + core * 8

    def y_copy(k, j):
        return remote(gat.at[ctx * 8 + resp], (y_send, y_recv), (k, j), peer_yz(k, j))

    def x_copy(k, j, n):
        first = line(k) + x * 2
        ref = gat.at[pl.ds(first, 2)] if n == 2 else gat.at[pl.ds(first + z, 1)]
        return remote(ref, (x_send, x_recv), (k, j), {"resp": ((x + j) % NX) * 2 + z})

    def z_copy(k, j):
        ref = gat.at[line(k) + ((x + NX - j) % NX) * 2 + z]
        return remote(ref, (z_send, z_recv), (k, j), {"resp": x * 2 + 1 - z})

    def s_copy(k):
        return remote(gat.at[pl.ds(line(k), 8)], (s_send, s_recv), (k,), {"ctx": y * 2 + 1 - core})

    def at_distance(n):
        return lax.rem((n + 1) // 2 * (n % 2) + (NY - n // 2) * (1 - n % 2), NY)

    def loop(first, last, step):
        def body(n, c):
            step(at_distance(n))
            return c

        lax.fori_loop(first, last, body, 0)

    def send_near(k):
        for j in (2, 1, 3):
            x_copy(k, j, 1).start()
        z_copy(k, 0).start()

    def pass_near(k):
        y_copy(k, 0).wait_recv()
        send_near(k)

    def pass_far(k):
        for j in range(2):
            y_copy(k, j).wait_recv()
        for j in (2, 1, 3):
            x_copy(k, j, 2).start()

    def pass_z(k):
        for j in (1, 3, 2):
            x_copy(k, j, 1).wait_recv()
            z_copy(k, j).start()

    def line_near(k):
        for j in range(NX):
            z_copy(k, j).wait_recv()
        s_copy(k).start()

    def line_far(k):
        for j in (1, 3, 2):
            x_copy(k, j, 2).wait_recv()
        s_copy(k).start()

    def start_far(n, c):
        k = at_distance(NY - 1 - n)
        for j in range(2):
            y_copy(k, j).start()
        return c

    lax.fori_loop(0, NY - NEAR, start_far, 0)
    loop(1, NEAR, lambda k: y_copy(k, 0).start())
    send_near(0)
    run_own(CHUNKS // 2, CHUNKS, 256)
    loop(1, NEAR, pass_near)
    pass_z(0)
    loop(NEAR, NY, pass_far)
    loop(1, NEAR, pass_z)
    loop(0, NEAR, line_near)
    loop(NEAR, NY, line_far)

    def end_near(k):
        for j in range(1, NX):
            x_copy(k, j, 1).wait_send()
        for j in range(NX):
            z_copy(k, j).wait_send()
        s_copy(k).wait()

    def end_far(k):
        for j in range(2):
            y_copy(k, j).wait_send()
        for j in range(1, NX):
            x_copy(k, j, 2).wait_send()
        s_copy(k).wait()

    loop(1, NEAR, lambda k: y_copy(k, 0).wait_send())
    loop(0, NEAR, end_near)
    loop(NEAR, NY, end_far)

    block_ids = lax.broadcasted_iota(jnp.int32, (1, 128), 1)
    first_block = jnp.min(jnp.where(mask_ref[...] == 1, block_ids, WINDOW))
    win = gat[pl.ds(first_block, WINDOW)].astype(f32)
    wk[pl.ds(0, 512), :] = jnp.concatenate([win[:, 0:8], win[:, 8:16]], axis=2).reshape(512, 256).astype(bf16)
    wv[pl.ds(0, 512), :] = jnp.concatenate([win[:, 16:24], win[:, 24:32]], axis=2).reshape(512, 256).astype(bf16)

    low4 = lax.broadcasted_iota(jnp.int32, (32, 8, 128), 1) < 4

    def rest(part4):
        part4 = part4.reshape(32, 2, 8, 128)
        b0, b1 = part4[:, 0], part4[:, 1]
        left = jnp.where(low4, b0, pltpu.roll(b1, 4, 1))
        right = jnp.where(low4, pltpu.roll(b0, 4, 1), b1)
        return jnp.concatenate([left, right], axis=2).reshape(256, 256).astype(bf16)

    wk[pl.ds(512, 256), :] = rest(win[:, 32:40])
    wv[pl.ds(512, 256), :] = rest(win[:, 40:48])

    acc[...] = jnp.zeros_like(acc)

    def prompt_scores(i, slot):
        rows = pl.ds(pl.multiple_of(i * R, R), R)
        s = dot_t(qe[rows, :], wk[...])
        s2[slot] = s
        top = s[:, :128]
        for j in range(1, 6):
            top = jnp.maximum(top, s[:, j * 128 : (j + 1) * 128])
        m2[slot] = jnp.maximum(m1[rows, :], jnp.broadcast_to(jnp.max(top, axis=1, keepdims=True), (R, 128)))

    def prompt_values(i, slot):
        rows = pl.ds(pl.multiple_of(i * R, R), R)
        g2 = ge[rows, :]
        mo, m = m1[rows, :], m2[slot]
        cols = [jnp.exp2((s2[slot, :, pl.ds(j * 128, 128)] - m) * C) for j in range(6)]
        p = jnp.concatenate(cols, axis=1)
        alpha = jnp.exp2((mo - m) * C)
        tot = l1[rows, :] * alpha
        for j in range(6):
            tot = tot + p[:, j * 128 : (j + 1) * 128]
        inv = 1.0 / jnp.sum(tot, axis=1, keepdims=True)
        mixed = (a1[rows, :] * alpha + pick(dot(p.astype(bf16), wv[...]))) * inv
        o_ref[rows, :] = mixed.astype(bf16)
        g = (g2[:, :128] + g2[:, 128:]).astype(f32)
        inner = jnp.sum(g * mixed, axis=1, keepdims=True)
        ed = e0[rows, :] * (alpha * inv) * (d0[rows, :] - jnp.where(lane < 64, 0.0, inner))
        ed = ed.astype(bf16)
        acc[...] += dot(turned[:, rows], jnp.concatenate([ed * lo, ed * hi], axis=1))

    staggered(prompt_scores, prompt_values, 0, CHUNKS)

    sums = acc[...].T.astype(bf16)
    part[pl.ds(0, 4)] = sums[64:128, 128:].reshape(4, 16, 128)
    part[pl.ds(4, 4)] = sums[192:, 128:].reshape(4, 16, 128)
    part[pl.ds(8, 4)] = sums[:64, :128].reshape(4, 16, 128)
    part[pl.ds(12, 4)] = sums[128:192, :128].reshape(4, 16, 128)

    seat = resp * 2 + core

    def r1_copy(k):
        return pltpu.make_async_remote_copy(
            src_ref=part.at[(seat + k) % 16], dst_ref=r1.at[k], send_sem=r1_send.at[k], recv_sem=r1_recv.at[k],
            device_id=peer_xzc(k), device_id_type=MESH,
        )

    def r2_copy(k):
        return pltpu.make_async_remote_copy(
            src_ref=r2.at[y], dst_ref=r2.at[y], send_sem=r2_send.at[k], recv_sem=r2_recv.at[k],
            device_id=peer_yz(k, 0), device_id_type=MESH,
        )

    def r3_copy(k):
        return pltpu.make_async_remote_copy(
            src_ref=fin.at[seat], dst_ref=fin.at[seat], send_sem=r3_send.at[k], recv_sem=r3_recv.at[k],
            device_id=peer_xzc(k), device_id_type=MESH,
        )

    def each(copy, n, what):
        def step(i, c):
            getattr(copy(lax.rem(i + n // 2, n) + i // (n // 2)), what)()
            return c

        lax.fori_loop(0, n - 1, step, 0)

    each(r1_copy, 16, "start")
    total = part[seat].astype(f32)
    each(r1_copy, 16, "wait_recv")
    for k in range(1, 16):
        total = total + r1[k].astype(f32)
    r2[y] = total.astype(bf16)
    each(r2_copy, 8, "start")
    each(r2_copy, 8, "wait_recv")
    total = r2[0].astype(f32)
    for k in range(1, 8):
        total = total + r2[k].astype(f32)
    fin[seat] = total.astype(bf16)
    each(r3_copy, 16, "start")
    each(r3_copy, 16, "wait_recv")
    for head in range(2):
        dst = pl.ds(head, 64, stride=2)
        gk_ref[dst, :] = fin[pl.ds(4 * head, 4)].astype(f32).reshape(64, 128) * (128.0 ** (-0.5))
        gv_ref[dst, :] = fin[pl.ds(8 + 4 * head, 4)].astype(f32).reshape(64, 128)
    each(r1_copy, 16, "wait_send")
    each(r2_copy, 8, "wait_send")
    each(r3_copy, 16, "wait_send")


def place(o_ref, k_ref, v_ref, out_ref, gk_ref, gv_ref, sem):
    n = ROWS // 4
    copies = [pltpu.make_async_copy(k_ref, gk_ref, sem.at[4]), pltpu.make_async_copy(v_ref, gv_ref, sem.at[5])]
    for i in range(4):
        rows = pl.ds(i * n, n)
        copies.append(pltpu.make_async_copy(o_ref.at[rows], out_ref.at[rows], sem.at[i]))
    for copy in copies:
        copy.start()
    for copy in copies:
        copy.wait()


def per_device(
    queries, prompt_k, prompt_v, resp_k, resp_v, prefix_k, prefix_v, d_out, shard_mask, resp_lengths, prefix_count
):
    vm = pl.BlockSpec(memory_space=pltpu.VMEM)
    hbm = pl.BlockSpec(memory_space=pltpu.HBM)
    vmem, dma = pltpu.VMEM, pltpu.SemaphoreType.DMA
    out, gk, gv = pl.pallas_call(
        kernel,
        out_shape=[vmem((ROWS, 128), bf16), vmem((128, 128), f32), vmem((128, 128), f32)],
        in_specs=[hbm] * 11,
        out_specs=[vm] * 3,
        scratch_shapes=[
            vmem((512, 128), f32), vmem((384, 256), bf16), vmem((384, 256), bf16), vmem((128, 256), bf16),
            vmem((ROWS, 128), bf16), vmem((ROWS, 128), bf16), vmem((512, 128), bf16), vmem((512, 128), bf16),
            vmem((128, 128), bf16), vmem((128, 128), bf16), vmem((2 * BLOCK, 128), bf16), vmem((2 * BLOCK, 128), bf16),
            vmem((1, 128), jnp.int32), pltpu.SMEM((1,), jnp.int32), pltpu.SMEM((1,), jnp.int32),
            vmem((ROWS, 256), bf16), vmem((ROWS, 256), bf16),
            vmem((ROWS, 128), f32), vmem((ROWS, 128), f32), vmem((ROWS, 128), f32),
            vmem((ROWS, 128), f32), vmem((ROWS, 128), f32),
            vmem((768, 256), bf16), vmem((768, 256), bf16),
            vmem((2, R, 384), f32), vmem((2, R, 768), f32), vmem((2, R, 128), f32),
            vmem((128, 48, 128), bf16),
            vmem((16, 16, 128), bf16), vmem((16, 16, 128), bf16), vmem((8, 16, 128), bf16), vmem((16, 16, 128), bf16),
            vmem((256, 256), f32), vmem((256, ROWS), bf16),
            dma((11,)), dma((8, 2)), dma((8, 2)), dma((8, 4)), dma((8, 4)), dma((8, 4)), dma((8, 4)),
            dma((8,)), dma((8,)), dma((16,)), dma((16,)), dma((8,)), dma((8,)), dma((16,)), dma((16,)),
        ],
        compiler_params=pltpu.CompilerParams(
            collective_id=0, has_side_effects=True, vmem_limit_bytes=60 << 20
        ),
    )(
        queries.reshape(ROWS, 128), d_out.reshape(ROWS, 128), resp_k.reshape(512, 128), resp_v.reshape(512, 128),
        prefix_k.reshape(128, 128), prefix_v.reshape(128, 128), prompt_k.reshape(2 * BLOCK, 128),
        prompt_v.reshape(2 * BLOCK, 128), shard_mask, resp_lengths, prefix_count,
    )
    out, gk, gv = pl.pallas_call(
        place,
        out_shape=[
            jax.ShapeDtypeStruct((ROWS, 128), bf16),
            jax.ShapeDtypeStruct((128, 128), f32),
            jax.ShapeDtypeStruct((128, 128), f32),
        ],
        in_specs=[vm] * 3,
        out_specs=[hbm] * 3,
        scratch_shapes=[dma((6,))],
        compiler_params=pltpu.CompilerParams(vmem_limit_bytes=16 << 20),
    )(out, gk, gv)
    return out.reshape(256, 16, 128), gk.reshape(64, 2, 128), gv.reshape(64, 2, 128)


def solution(mesh):
    tokens = P(("ctx", "resp"), "head", None)
    prefix = P(None, "head", None)
    in_specs = (
        tokens, tokens, tokens, tokens, tokens, prefix, prefix, tokens,
        P(("ctx", "resp"), None), P(("ctx", "resp")), P(),
    )
    return jax.shard_map(
        per_device, mesh=mesh, in_specs=in_specs, out_specs=(tokens, prefix, prefix), check_vma=False
    )
```
